32 devices in a mesh: groups: 2 (over x), date: 16 (over z, y, core).
Axes of the slice: x: 2, y: 2, z: 4, core: 2. Of those that a mesh axis runs over, the one named last changes fastest.
Arguments:
- images: float32 [32, 2, 64, 2560], P(('groups', 'date')), parts along dimension 0, may hold values from -16 to 16
- height_phase: float32 [128, 2560], P(('groups', 'date')), parts along dimension 0, may hold values from -4 to 4
- baseline: float32 [32], P('groups'), parts along dimension 0, may hold values from -0.6 to 0.6
- pair_list: int32 [32, 2], replicated, may hold values from 0 to 15, as said below
- pair_owner: int32 [32, 1], replicated, may hold values from 0 to 15; in each aligned block of 32 rows (0 to 31, 32 to 63, ...) at most 4 rows name the same one
Outputs:
- interferogram: float32 [128, 2, 16, 128], P(('groups', 'date')), parts along dimension 0
- coherence: float32 [128, 16, 128], P(('groups', 'date')), parts along dimension 0
The draws below stay inside these ranges and needn't reach their ends.
There are 2 independent parts, one for each index of `groups`. The reference program is written for one: setup_inputs(seed, part) draws one part's arguments, and reference() takes and returns one part's arrays. A program takes and returns all parts, laid end to end along the dimension named above; an argument that names none is the same for every part. Nothing has to cross between parts.
Inputs may be any that keep to these rules, and one draw needn't show every extreme that they name: `pair_list`: each row is (r, s) with r < s <= r + 4; some pair has s = r + 4. `pair_owner`: every index owns at least one pair and at most 4 pairs; some index owns exactly 4.
All inputs are finite; a program needn't handle non-finite values.
Results may differ from the reference program's by a relative error of at most 0.00007.
Values sent between devices are 32-bit elements; how exact they have to be, the bound alone decides.
No kernel may reach another device: no remote copies, remote signals or barrier semaphores. Data moves between devices by JAX's collectives and lax.ppermute only.
A program may use at most 128 MiB of HBM per device.

```python
import math
import jax
import jax.numpy as jnp
import numpy as np
from jax import lax

LOOK_ROWS = 4
LOOK_COLS = 20
BAND = 4
CAP = 4
COLS = 2560
DATES = 16
PAIRS = 32
ROWS = 64
N_DATE = 16


def draw_images(key, part):
    common = jax.random.normal(jax.random.fold_in(key, 101), (2, ROWS, COLS), jnp.float32)
    noise = jax.random.normal(jax.random.fold_in(key, 102), (DATES, 2, ROWS, COLS), jnp.float32)
    spread = math.log(10.0) / 4.0
    low_rho = 0.3
    high_rho = 0.95
    row_scale = jnp.exp(jax.random.uniform(jax.random.fold_in(key, 105), (ROWS,), jnp.float32, -spread, spread))
    col_scale = jnp.exp(jax.random.uniform(jax.random.fold_in(key, 106), (COLS,), jnp.float32, -spread, spread))
    amplitude = row_scale[:, None] * col_scale[None, :]
    rho_value = jax.random.uniform(jax.random.fold_in(key, 107), (DATES,), jnp.float32, low_rho, high_rho)
    angle_value = jax.random.uniform(jax.random.fold_in(key, 108), (DATES,), jnp.float32, -math.pi, math.pi)
    cosine = jnp.cos(angle_value)[:, None, None]
    sine_part = jnp.sin(angle_value)[:, None, None]
    common_real = cosine * common[0][None] - sine_part * common[1][None]
    common_imag = sine_part * common[0][None] + cosine * common[1][None]
    rest = jnp.sqrt(1.0 - rho_value * rho_value)[:, None, None]
    rho_wide = rho_value[:, None, None]
    real_part = amplitude[None] * (rho_wide * common_real + rest * noise[:, 0])
    imag_part = amplitude[None] * (rho_wide * common_imag + rest * noise[:, 1])
    return jnp.clip(jnp.stack([real_part, imag_part], axis=1), -16.0, 16.0).astype(jnp.float32)


def draw_pair_list(key, part):
    first_date = jax.random.randint(jax.random.fold_in(key, 201), (PAIRS,), 0, DATES - BAND, jnp.int32)
    distance = jax.random.randint(jax.random.fold_in(key, 202), (PAIRS,), 1, BAND + 1, jnp.int32)
    position = jnp.arange(PAIRS, dtype=jnp.int32)
    distance = jnp.where(position == 0, BAND, distance)
    return jnp.stack([first_date, first_date + distance], axis=1).astype(jnp.int32)


def shard_levels(own_key, extent, cuts, smallest, largest):
    factor_of = 1.0
    for axis_at, parts in cuts:
        draws = jax.random.uniform(jax.random.fold_in(jax.random.fold_in(own_key, 6), axis_at), (parts,), jnp.float32, smallest / len(cuts), largest / len(cuts))
        factor_of = factor_of * jnp.repeat(jnp.exp(draws), extent[axis_at] // parts).reshape((-1,) + (1,) * (len(extent) - 1 - axis_at))
    return factor_of


def shared_out(own_key, own, number, rows, amount, top, limit, slope):
    sequence = jax.random.permutation(own_key, amount)
    crowded, ordinary = shares(amount, rows * top, limit, slope, True), shares(amount, rows * top, limit, slope, False)
    places = jnp.arange(amount)

    def named(lengths, rotation):
        used = int((lengths > 0).sum())
        fixed = max(1, used // 4)
        passed = fixed + (places - fixed + rotation * (used - fixed)) % max(1, amount - fixed)
        return jnp.zeros((amount,), jnp.int32).at[sequence[jnp.where(places < fixed, places, passed)]].set(jnp.asarray(lengths, jnp.int32))

    lengths = jnp.where(number % 4 == 0, named(crowded, number // 4), named(ordinary, number - number // 4 - 1))
    mixed = jax.random.permutation(jax.random.fold_in(own, 3), amount)
    giver, sink = mixed[0:amount // 2 * 2:2], mixed[1:amount // 2 * 2:2]
    slack = jnp.minimum(lengths[giver] - 1, limit - lengths[sink]) // 2
    slack = jnp.where((giver == sequence[0]) | (sink == sequence[0]) | (lengths[sink] == 0), 0, jnp.maximum(slack, 0))
    passed = jax.random.randint(jax.random.fold_in(own, 4), (amount // 2,), 0, 1 << 20) % (slack + 1)
    lengths = lengths.at[giver].add(-passed).at[sink].add(passed)
    labels = jnp.searchsorted(jnp.cumsum(lengths), jnp.arange(rows * top), side="right").astype(jnp.int32)
    grid = labels.reshape(top, rows).T
    grid = grid[jax.random.permutation(jax.random.fold_in(own, 1), rows)]
    rotation = jax.random.randint(jax.random.fold_in(own, 2), (rows, 1), 0, top)
    return jnp.take_along_axis(grid, (jnp.arange(top)[None, :] + rotation) % top, axis=1)


def shares(number_of, total, bound, skew, full):
    weights = [(1 << 20) // math.isqrt(standing ** skew) + 1 for standing in range(1, number_of + 1)]
    largest = bound if full else min(bound, max(-(-total // number_of), total * weights[0] // sum(weights)))
    least = 1 if total - largest >= number_of - 1 else 0
    counts, spare = [largest] + [least] * (number_of - 1), total - largest - least * (number_of - 1)
    while spare > 0:
        free = [i for i in range(1, number_of) if counts[i] < largest] or [i for i in range(1, number_of) if counts[i] < bound]
        mass, remaining = sum([weights[i] for i in free]), spare
        for i in free:
            extra = min(bound - counts[i], max(1, remaining * weights[i] // mass), spare)
            counts[i] = counts[i] + extra
            spare = spare - extra
    return np.array(counts)


def scatter_about(rng, extent, scale, limit, pieces=(), held_as=jnp.bfloat16):
    values = scale * jax.random.normal(rng, extent, jnp.float32)
    if pieces:
        values = values * shard_levels(rng, extent, pieces, -0.22, 0.18)
    return jnp.clip(values, -limit, limit).astype(held_as)


def setup_inputs(seed: int = 0, part: int = 0) -> dict:
    splits = jax.random.split(jax.random.key(seed), 6)
    part_splits = jax.random.split(jax.random.fold_in(splits[5], part), 6)
    images = draw_images(jax.random.fold_in(jax.random.fold_in(splits[5], part), 71), part)
    height_phase = scatter_about(part_splits[1], (ROWS, COLS), 1.0, 4.0, ((0, 16),), jnp.float32)
    baseline = jnp.clip(jax.random.uniform(part_splits[2], (DATES,), jnp.float32, -0.6, 0.6), -0.6, 0.6)
    pair_list = draw_pair_list(jax.random.fold_in(splits[5], 71), part)
    pair_owner_keys = jax.random.split(jax.random.fold_in(splits[4], 1), PAIRS // PAIRS)
    pair_owner_turns = jax.random.permutation(jax.random.fold_in(splits[4], 3), PAIRS // PAIRS)
    pair_owner = jax.vmap(lambda own, number: shared_out(jax.random.fold_in(splits[4], 2), own, number, PAIRS, N_DATE, 1, CAP, 2))(pair_owner_keys, pair_owner_turns).reshape((PAIRS, 1))
    return {"images": images, "height_phase": height_phase, "baseline": baseline, "pair_list": pair_list, "pair_owner": pair_owner}


EPSILON = 1e-06

def multilook(values):
    values_shape = values.shape
    grouped = values.reshape(values_shape[:-2] + (values_shape[-2] // LOOK_ROWS, LOOK_ROWS, values_shape[-1] // LOOK_COLS, LOOK_COLS))
    return lax.optimization_barrier(jnp.mean(grouped, axis=(-3, -1)))

def flatten_phase(images, factors, height_phase):
    phase_angle = factors[:, None, None] * height_phase[None]
    cosine = jnp.cos(phase_angle)
    sine_part = jnp.sin(phase_angle)
    real_part = images[:, 0] * cosine - images[:, 1] * sine_part
    imag_part = images[:, 0] * sine_part + images[:, 1] * cosine
    return (real_part, imag_part)

def slot_of(pair_owner):
    owners = pair_owner[:, 0]
    position = jnp.arange(owners.shape[0], dtype=jnp.int32)
    earlier = (owners[:, None] == owners[None, :]) & (position[:, None] > position[None, :])
    return (owners * CAP + lax.optimization_barrier(jnp.sum(earlier.astype(jnp.int32), axis=1))).astype(jnp.int32)

def reference(images, height_phase, baseline, pair_list, pair_owner):
    real_part, imag_part = flatten_phase(images, baseline, height_phase)
    power_map = multilook(real_part * real_part + imag_part * imag_part)

    def one_pair(pair_row):
        first_date = pair_row[0]
        second_date = pair_row[1]
        first_real = real_part[first_date]
        first_imag = imag_part[first_date]
        second_real = real_part[second_date]
        second_imag = imag_part[second_date]
        look_real = multilook(first_real * second_real + first_imag * second_imag)
        look_imag = multilook(first_imag * second_real - first_real * second_imag)
        denominator = jnp.sqrt((power_map[first_date] + EPSILON) * (power_map[second_date] + EPSILON))
        coherence = jnp.sqrt(look_real * look_real + look_imag * look_imag) / denominator
        return jnp.stack([look_real, look_imag, coherence])
    results = lax.map(one_pair, pair_list)
    slot_index = slot_of(pair_owner)
    filled = jnp.zeros((CAP * N_DATE,) + results.shape[1:], jnp.float32).at[slot_index].set(results)
    return (filled[:, :2], filled[:, 2])
```

```python
import functools

import jax
import jax.numpy as jnp
from jax import lax
from jax.experimental import pallas as pl
from jax.experimental.pallas import tpu as pltpu
from jax.sharding import PartitionSpec as P

LOOK_ROWS = 4
LOOK_COLS = 20
BAND = 4
CAP = 4
EPSILON = 1e-06

LANES = 128
SUB = 8
ROW_SETS = SUB // LOOK_ROWS
KINDS = 3
SLOT_ROWS = KINDS * ROW_SETS
MIB = 1024 * 1024


def box_matrix(columns):
    position = jnp.arange(columns, dtype=jnp.int32)
    target = jnp.arange(columns // LOOK_COLS, dtype=jnp.int32)
    return (position[:, None] // LOOK_COLS == target[None, :]).astype(jnp.bfloat16)


def pack_kernel(half, place_ref, images_ref, packed_ref, *halo_refs):
    side = place_ref[0]
    lane = place_ref[1]
    columns = images_ref.shape[-1]
    upper = lax.broadcasted_iota(jnp.int32, (SUB, columns), 0) < LOOK_ROWS
    for part in range(2):
        for pair in range(half // 2):
            first = images_ref[0, part, pair * SUB : (pair + 1) * SUB, :]
            at = (pair + half // 2) * SUB
            second = images_ref[0, part, at : at + SUB, :]
            spot = slice(part * SUB, (part + 1) * SUB)
            packed_ref[2 * pair, spot, :] = jnp.where(
                upper, first, pltpu.roll(second, LOOK_ROWS, 0)
            )
            packed_ref[2 * pair + 1, spot, :] = jnp.where(
                upper, pltpu.roll(first, LOOK_ROWS, 0), second
            )
    for n, halo_ref in enumerate(halo_refs):
        target = n // BAND * BAND + jnp.bitwise_xor(lane, n % BAND)
        halo_ref[...] = packed_ref[jnp.where(side == 0, target, half // 2 + target)]


def table_kernel(blocks, factor_ref, upper_ref, lower_ref, cos_ref, sin_ref):
    groups = factor_ref.shape[0] // SUB

    def block(t, carry):
        column = pl.ds(pl.multiple_of(t * LANES, LANES), LANES)
        for b, phase_ref in enumerate((upper_ref, lower_ref)):
            for line in range(LOOK_ROWS):
                phase = phase_ref[line : line + 1, column]
                for group in range(groups):
                    factor = factor_ref[group * SUB : (group + 1) * SUB, :]
                    x = factor * phase
                    z = x * x
                    s = -1.0 / 39916800.0
                    for c in (362880.0, -5040.0, 120.0, -6.0, 1.0):
                        s = s * z + 1.0 / c
                    s = s * x
                    c = 1.0 / 479001600.0
                    for d in (-3628800.0, 40320.0, -720.0, 24.0, -2.0, 1.0):
                        c = c * z + 1.0 / d
                    twice = s + s
                    at = ((t * SUB + b * LOOK_ROWS + line) * groups + group) * SUB
                    spot = pl.ds(pl.multiple_of(at, SUB), SUB)
                    cos_ref[spot, :] = 1.0 - twice * s
                    sin_ref[spot, :] = twice * c
        return carry

    lax.fori_loop(0, blocks, block, 0)


def pair_kernel(
    half,
    blocks,
    pairs,
    place_ref,
    first_ref,
    second_ref,
    owner_ref,
    own_ref,
    *rest,
):
    halo_refs = rest[:BAND]
    cos_ref, sin_ref, box_ref, out_ref, raw_ref, sum_ref, result_ref, count_ref = rest[
        BAND:
    ]
    tiles = half // SUB
    groups = tiles + 1
    per_part = blocks * SUB
    per_date = 2 * per_part
    side = place_ref[0]
    lane = place_ref[1]
    low = side == 0
    halo_row = side * BAND
    raw_ref[...] = jnp.zeros_like(raw_ref)
    row_index = lax.broadcasted_iota(jnp.int32, (SUB, LANES), 0)
    masks = []
    shifts = []
    for k in range(1, BAND + 1):
        masks.append(
            jnp.where(low, row_index - k, SUB - 1 - k - row_index) >= 0
        )
        shifts.append(jnp.where(low, SUB - k, k))

    def partners(values, edge):
        found = []
        for tile in range(tiles):
            after = values[tile + 1] if tile + 1 < tiles else edge
            before = values[tile - 1] if tile > 0 else edge
            beside = edge if tiles == 1 else jnp.where(low, after, before)
            found.append(
                [
                    pltpu.roll(jnp.where(masks[k], values[tile], beside), shifts[k], 0)
                    for k in range(BAND)
                ]
            )
        return found

    def block(t, carry):
        line_at = pl.multiple_of(t * SUB, SUB)
        column = pl.ds(pl.multiple_of(t * LANES, LANES), LANES)
        for part in range(2):
            for i in range(BAND):
                row = halo_row + jnp.bitwise_xor(lane, i)
                raw_ref[part, pl.ds(row, SUB, stride=SUB), :] = halo_refs[i][
                    pl.ds(part * per_part + line_at, SUB), :
                ]

        def turned(line, group, real, imag):
            at = ((line_at + line) * groups + group) * SUB
            table = pl.ds(pl.multiple_of(at, SUB), SUB)
            cosine = cos_ref[table, :]
            sine_part = sin_ref[table, :]
            return real * cosine - imag * sine_part, real * sine_part + imag * cosine

        for b in range(ROW_SETS):
            sums = {}

            def add(key, term):
                sums[key] = sums[key] + term if key in sums else term

            for line in range(b * LOOK_ROWS, (b + 1) * LOOK_ROWS):
                span = slice(line * SUB, (line + 1) * SUB)
                edge_real, edge_imag = turned(
                    line, tiles, raw_ref[0, span, :], raw_ref[1, span, :]
                )
                add((1 + 2 * BAND, 0), edge_real * edge_real + edge_imag * edge_imag)
                reals = []
                imags = []
                for tile in range(tiles):
                    start = tile * SUB * per_date + line_at + line
                    real, imag = turned(
                        line,
                        tile,
                        own_ref[pl.ds(start, SUB, stride=per_date), :],
                        own_ref[pl.ds(start + per_part, SUB, stride=per_date), :],
                    )
                    add((0, tile), real * real + imag * imag)
                    reals.append(real)
                    imags.append(imag)
                other_reals = partners(reals, edge_real)
                other_imags = partners(imags, edge_imag)
                for tile in range(tiles):
                    for k in range(BAND):
                        other_real = other_reals[tile][k]
                        other_imag = other_imags[tile][k]
                        real = reals[tile]
                        imag = imags[tile]
                        add((1 + 2 * k, tile), real * other_real + imag * other_imag)
                        add((2 + 2 * k, tile), imag * other_real - real * other_imag)
            for (kind, tile), value in sums.items():
                at = (kind * tiles * ROW_SETS + b * (1 if kind > 2 * BAND else tiles) + tile) * SUB
                sum_ref[at : at + SUB, column] = value
        return carry

    lax.fori_loop(0, blocks, block, 0)

    rest_of = sum_ref[...]
    box = box_ref[...]
    looked = None
    for piece in range(3):
        rounded = rest_of.astype(jnp.bfloat16)
        part = jnp.dot(rounded, box, preferred_element_type=jnp.float32)
        looked = part if looked is None else looked + part
        if piece < 2:
            rest_of = rest_of - rounded.astype(jnp.float32)
    looked = looked * (1.0 / (LOOK_ROWS * LOOK_COLS))

    def rows_of(kind, b, tile):
        at = (kind * tiles * ROW_SETS + b * (1 if kind > 2 * BAND else tiles) + tile) * SUB
        return looked[at : at + SUB, :]

    sign = jnp.where(low, 1.0, -1.0)
    for b in range(ROW_SETS):
        powers = [rows_of(0, b, tile) for tile in range(tiles)]
        other_powers = partners(powers, rows_of(1 + 2 * BAND, b, 0))
        for tile in range(tiles):
            for k in range(BAND):
                look_real = rows_of(1 + 2 * k, b, tile)
                look_imag = rows_of(2 + 2 * k, b, tile) * sign
                coherence = jnp.sqrt(
                    look_real * look_real + look_imag * look_imag
                ) / jnp.sqrt((powers[tile] + EPSILON) * (other_powers[tile][k] + EPSILON))
                for kind, value in enumerate((look_real, look_imag, coherence)):
                    at = (k * half + tile * SUB) * SUB + kind * ROW_SETS + b
                    result_ref[pl.ds(at, SUB, stride=SUB), :] = value

    out_ref[...] = jnp.zeros_like(out_ref)

    def clear(o, carry):
        count_ref[o] = 0
        return carry

    lax.fori_loop(0, 2 * half, clear, 0)

    def place(p, carry):
        owner = owner_ref[p]
        taken = count_ref[owner]
        count_ref[owner] = taken + 1
        first = first_ref[p]
        second = second_ref[p]
        mine = jnp.where(low, first < half, second >= half)

        @pl.when(mine)
        def _():
            own = jnp.where(low, first, second - half)
            at = pl.multiple_of(((second - first - 1) * half + own) * SUB, SUB)
            out_ref[pl.ds((owner * CAP + taken) * SLOT_ROWS, SLOT_ROWS), :] = (
                result_ref[pl.ds(at, SUB), :][:SLOT_ROWS]
            )

        return carry

    lax.fori_loop(0, pairs, place, 0)


def collect_kernel(half, got_ref, look_ref, coherence_ref):
    per_device = CAP * SLOT_ROWS
    for tile in range(half // SUB):
        for slot in range(CAP):
            for kind in range(KINDS):
                for b in range(ROW_SETS):
                    at = tile * SUB * per_device + slot * SLOT_ROWS + kind * ROW_SETS + b
                    value = got_ref[pl.ds(at, SUB, stride=per_device), :]
                    at += half * per_device
                    value += got_ref[pl.ds(at, SUB, stride=per_device), :]
                    at = b * half + tile * SUB
                    if kind < 2:
                        look_ref[slot, kind, at : at + SUB, :] = value
                    else:
                        coherence_ref[slot, at : at + SUB, :] = value


def body(images, height_phase, baseline, pair_list, pair_owner):
    devices = lax.axis_size("date")
    half = devices // 2
    me = lax.axis_index("date")
    side = me // half
    lane = me % BAND
    rows, columns = images.shape[2:]
    blocks = columns // LANES
    pairs = pair_list.shape[0]
    tiles = half // SUB
    groups = tiles + 1
    assert images.shape[0] == 1 and rows == SUB * half and half % SUB == 0
    assert columns == blocks * LANES == LANES * LOOK_COLS
    vmem = pl.BlockSpec(memory_space=pltpu.VMEM)
    smem = pl.BlockSpec(memory_space=pltpu.SMEM)
    place = jnp.stack([side, lane]).astype(jnp.int32)

    block = jax.ShapeDtypeStruct((2 * SUB, columns), jnp.float32)
    packed, *edges = pl.pallas_call(
        functools.partial(pack_kernel, half),
        out_shape=[jax.ShapeDtypeStruct((half, 2 * SUB, columns), jnp.float32)]
        + [block] * (half // 2),
        in_specs=[smem, vmem],
        out_specs=[vmem] * (1 + half // 2),
        compiler_params=pltpu.CompilerParams(vmem_limit_bytes=24 * MIB),
        name="pack_lines",
    )(place, images)
    halves = [list(range(half)), list(range(half, devices))]
    own = lax.all_to_all(
        packed, "date", split_axis=0, concat_axis=0, tiled=True, axis_index_groups=halves
    )

    def as_rows(values):
        values = values.reshape(-1, SUB, blocks, LANES)
        return jnp.swapaxes(values, 1, 2).reshape(-1, LANES)

    across = lax.ppermute(
        height_phase, "date", [(k, (k + half) % devices) for k in range(devices)]
    )

    halos = []
    for i in range(BAND):
        arrived = None
        for g in range(half // 2 // BAND):
            steps = []
            for a in range(BAND):
                steps.append((half + a, half // 2 + BAND * g + (a ^ i)))
                steps.append((half - BAND + a, half + BAND * g + (a ^ i)))
            got = lax.ppermute(edges[BAND * g + i], "date", steps)
            arrived = got if arrived is None else arrived + got
        halos.append(as_rows(arrived))

    low = side == 0
    upper_phase = jnp.where(low, height_phase, across)
    lower_phase = jnp.where(low, across, height_phase)
    own_factors = lax.dynamic_slice_in_dim(baseline, side * half, half)
    edge_factors = lax.dynamic_slice_in_dim(
        baseline, jnp.where(low, half, half - SUB), SUB
    )
    factors = 0.5 * jnp.concatenate([own_factors, edge_factors])
    factors = jnp.broadcast_to(factors[:, None], (half + SUB, LANES))
    table = jax.ShapeDtypeStruct((blocks * SUB * groups * SUB, LANES), jnp.float32)
    cosine, sine_part = pl.pallas_call(
        functools.partial(table_kernel, blocks),
        out_shape=[table, table],
        in_specs=[vmem] * 3,
        out_specs=[vmem] * 2,
        compiler_params=pltpu.CompilerParams(vmem_limit_bytes=24 * MIB),
        name="phase_tables",
    )(factors, upper_phase, lower_phase)

    sums = ((1 + 2 * BAND) * tiles + 1) * ROW_SETS * SUB
    slot_rows = devices * CAP * SLOT_ROWS
    buffer = pl.pallas_call(
        functools.partial(pair_kernel, half, blocks, pairs),
        out_shape=jax.ShapeDtypeStruct((slot_rows, LANES), jnp.float32),
        in_specs=[smem] * 4 + [vmem] * (BAND + 4),
        out_specs=vmem,
        scratch_shapes=[
            pltpu.VMEM((2, SUB * SUB, LANES), jnp.float32),
            pltpu.VMEM((sums, columns), jnp.float32),
            pltpu.VMEM((BAND * half * SUB, LANES), jnp.float32),
            pltpu.SMEM((devices,), jnp.int32),
        ],
        compiler_params=pltpu.CompilerParams(vmem_limit_bytes=(12 + 12 * tiles) * MIB),
        name="pair_products",
    )(
        place,
        pair_list[:, 0],
        pair_list[:, 1],
        pair_owner[:, 0],
        as_rows(own.reshape(half * 2, SUB, columns)),
        *halos,
        cosine,
        sine_part,
        box_matrix(columns),
    )
    delivered = lax.all_to_all(
        buffer.reshape(devices, CAP * SLOT_ROWS, LANES),
        "date",
        split_axis=0,
        concat_axis=0,
        tiled=True,
    )
    look_rows = rows // LOOK_ROWS
    return pl.pallas_call(
        functools.partial(collect_kernel, half),
        out_shape=(
            jax.ShapeDtypeStruct((CAP, 2, look_rows, LANES), jnp.float32),
            jax.ShapeDtypeStruct((CAP, look_rows, LANES), jnp.float32),
        ),
        in_specs=[vmem],
        out_specs=(vmem, vmem),
        compiler_params=pltpu.CompilerParams(vmem_limit_bytes=16 * MIB),
        name="collect_slots",
    )(delivered.reshape(slot_rows, LANES))


def solution(mesh):
    in_specs = (
        P(("groups", "date"), None, None, None),
        P(("groups", "date"), None),
        P("groups"),
        P(),
        P(),
    )
    out_specs = (P(("groups", "date"), None, None, None), P(("groups", "date"), None, None))
    return jax.shard_map(body, mesh=mesh, in_specs=in_specs, out_specs=out_specs, check_vma=False)
```

```python
import functools

import jax
import jax.numpy as jnp
from jax import lax
from jax.experimental import pallas as pl
from jax.experimental.pallas import tpu as pltpu
from jax.sharding import PartitionSpec as P

LOOK_ROWS = 4
LOOK_COLS = 20
BAND = 4
CAP = 4
EPSILON = 1e-06

LANES = 128
SUB = 8
ROW_SETS = SUB // LOOK_ROWS
KINDS = 3
SLOT_ROWS = KINDS * ROW_SETS
BOX_PARTS = 4
MIB = 1024 * 1024


SINE = (1.0, -0.1666666567325592, 0.00833327230066061, -0.00019829686789307743, 2.665147349034669e-06)
COSINE = (1.0, -0.49999988079071045, 0.041666001081466675, -0.001387619529850781, 2.3807961042621173e-05)


def cosine_and_sine(x):
    z = x * x
    s = SINE[-1]
    for c in SINE[-2::-1]:
        s = s * z + c
    s = s * x
    c = COSINE[-1]
    for d in COSINE[-2::-1]:
        c = c * z + d
    twice = s + s
    return 1.0 - twice * s, twice * c


def edge_kernel(half, packed_ref, *rest):
    edge_refs = rest[: half // 2]
    sem = rest[half // 2]
    me = lax.axis_index("date")
    lane = lax.rem(me, BAND)
    first = jnp.where(me < half, 0, half // 2)
    arriving = []
    for n, edge_ref in enumerate(edge_refs):
        target = first + n // BAND * BAND + jnp.bitwise_xor(lane, n % BAND)
        arriving.append(
            pltpu.make_async_copy(packed_ref.at[target], edge_ref, sem.at[n])
        )
        arriving[-1].start()
    for copy in arriving:
        copy.wait()


def pair_kernel(half, blocks, pairs, place_ref, factor_ref, phase_ref, own_ref, *rest):
    halo_refs = rest[:BAND]
    out_ref, raw_ref, sum_ref, box_ref, result_ref = rest[BAND:]
    tiles = half // SUB
    per_part = blocks * SUB
    per_date = 2 * per_part
    side = place_ref[0]
    lane = place_ref[1]
    low = side == 0
    row_index = lax.broadcasted_iota(jnp.int32, (SUB, LANES), 0)
    masks = []
    shifts = []
    for k in range(1, BAND + 1):
        masks.append(
            jnp.where(low, row_index - k, SUB - 1 - k - row_index) >= 0
        )
        shifts.append(jnp.where(low, SUB - k, k))

    def partners(values, edge):
        found = []
        for tile in range(tiles):
            after = values[tile + 1] if tile + 1 < tiles else edge
            before = values[tile - 1] if tile > 0 else edge
            beside = edge if tiles == 1 else jnp.where(low, after, before)
            found.append(
                [
                    pltpu.roll(jnp.where(masks[k], values[tile], beside), shifts[k], 0)
                    for k in range(BAND)
                ]
            )
        return found

    box_columns = box_ref.shape[0]
    offset = lax.broadcasted_iota(
        jnp.int32, (box_columns, LANES), 0
    ) - LOOK_COLS * lax.broadcasted_iota(jnp.int32, (box_columns, LANES), 1)
    inside = jnp.where((offset >= 0) & (offset < LOOK_COLS), 1.0, 0.0)
    box_ref[...] = inside.astype(jnp.bfloat16)

    def turned(angle, real, imag):
        cosine, sine_part = cosine_and_sine(angle)
        return real * cosine - imag * sine_part, real * sine_part + imag * cosine

    first_row = row_index < BAND
    to_even = SUB // 2 * side
    to_odd = SUB // 2 - to_even
    edge_kind = 1 + 2 * BAND

    def block(t, carry):
        line_at = pl.multiple_of(t * SUB, SUB)
        column = pl.ds(pl.multiple_of(t * LANES, LANES), LANES)
        for part in range(2):
            for i in range(BAND):
                row = jnp.bitwise_xor(lane, i)
                raw_ref[part, pl.ds(row, SUB, stride=BAND), :] = halo_refs[i][
                    pl.ds(part * per_part + line_at, SUB), :
                ]
        for b in range(ROW_SETS):
            sums = {}

            def add(key, term):
                sums[key] = sums[key] + term if key in sums else term

            for even in range(b * LOOK_ROWS, (b + 1) * LOOK_ROWS, 2):
                phases = [phase_ref[line : line + 1, column] for line in (even, even + 1)]
                span = slice(even * BAND, even * BAND + SUB)
                edge = turned(
                    factor_ref[tiles * SUB :, :] * jnp.where(first_row, *phases),
                    raw_ref[0, span, :],
                    raw_ref[1, span, :],
                )
                add((edge_kind, 0), edge[0] * edge[0] + edge[1] * edge[1])
                for line in (even, even + 1):
                    to_place = to_even if line == even else to_odd
                    edge_real, edge_imag = [pltpu.roll(v, to_place, 0) for v in edge]
                    reals = []
                    imags = []
                    for tile in range(tiles):
                        start = tile * SUB * per_date + line_at + line
                        real, imag = turned(
                            factor_ref[tile * SUB : (tile + 1) * SUB, :]
                            * phases[line - even],
                            own_ref[pl.ds(start, SUB, stride=per_date), :],
                            own_ref[pl.ds(start + per_part, SUB, stride=per_date), :],
                        )
                        add((0, tile), real * real + imag * imag)
                        reals.append(real)
                        imags.append(imag)
                    other_reals = partners(reals, edge_real)
                    other_imags = partners(imags, edge_imag)
                    for tile in range(tiles):
                        for k in range(BAND):
                            other_real = other_reals[tile][k]
                            other_imag = other_imags[tile][k]
                            real = reals[tile]
                            imag = imags[tile]
                            add((1 + 2 * k, tile), real * other_real + imag * other_imag)
                            add((2 + 2 * k, tile), imag * other_real - real * other_imag)
            for (kind, tile), value in sums.items():
                at = sum_row(kind, b, tile)
                sum_ref[at : at + SUB, column] = value
        return carry

    def sum_row(kind, b, tile):
        return (kind * tiles * ROW_SETS + b * (1 if kind == edge_kind else tiles) + tile) * SUB

    lax.fori_loop(0, blocks, block, 0)

    box = box_ref[...]
    looked = None
    for part in range(sum_ref.shape[1] // box_columns):
        rest_of = sum_ref[:, part * box_columns : (part + 1) * box_columns]
        parts = None
        for piece in range(3):
            rounded = rest_of.astype(jnp.bfloat16)
            value = jnp.dot(rounded, box, preferred_element_type=jnp.float32)
            parts = value if parts is None else parts + value
            if piece < 2:
                rest_of = rest_of - rounded.astype(jnp.float32)
        if part:
            parts = pltpu.roll(parts, part * (box_columns // LOOK_COLS), 1)
        looked = parts if looked is None else looked + parts
    looked = looked * (1.0 / (LOOK_ROWS * LOOK_COLS))

    def rows_of(kind, b, tile):
        at = sum_row(kind, b, tile)
        return looked[at : at + SUB, :]

    sign = jnp.where(low, 1.0, -1.0)
    for b in range(ROW_SETS):
        powers = [rows_of(0, b, tile) for tile in range(tiles)]
        edge_power = rows_of(edge_kind, b, 0)
        other_powers = partners(powers, edge_power + pltpu.roll(edge_power, SUB // 2, 0))
        for tile in range(tiles):
            for k in range(BAND):
                look_real = rows_of(1 + 2 * k, b, tile)
                look_imag = rows_of(2 + 2 * k, b, tile) * sign
                coherence = jnp.sqrt(
                    look_real * look_real + look_imag * look_imag
                ) / jnp.sqrt((powers[tile] + EPSILON) * (other_powers[tile][k] + EPSILON))
                for kind, value in enumerate((look_real, look_imag, coherence)):
                    at = (k * half + tile * SUB) * SUB + kind * ROW_SETS + b
                    result_ref[pl.ds(at, SUB, stride=SUB), :] = value

    out_ref[...] = jnp.zeros_like(out_ref)
    result_ref[BAND * half * SUB :, :] = jnp.zeros((SUB, LANES), jnp.float32)
    for p in range(pairs):
        taken = pl.multiple_of(place_ref[2 + pairs + p] * SUB, SUB)
        out_ref[pl.ds(place_ref[2 + p] * SLOT_ROWS, SLOT_ROWS), :] = result_ref[
            pl.ds(taken, SUB), :
        ][:SLOT_ROWS]


def collect_kernel(half, got_ref, look_ref, coherence_ref):
    per_device = CAP * SLOT_ROWS
    for tile in range(half // SUB):
        for slot in range(CAP):
            for kind in range(KINDS):
                for b in range(ROW_SETS):
                    at = tile * SUB * per_device + slot * SLOT_ROWS + kind * ROW_SETS + b
                    value = got_ref[pl.ds(at, SUB, stride=per_device), :]
                    at += half * per_device
                    value += got_ref[pl.ds(at, SUB, stride=per_device), :]
                    spot = pl.ds(tile * SUB * ROW_SETS + b, SUB, stride=ROW_SETS)
                    if kind < 2:
                        look_ref[slot, kind, spot, :] = value
                    else:
                        coherence_ref[slot, spot, :] = value


def body(images, height_phase, baseline, pair_list, pair_owner):
    devices = lax.axis_size("date")
    half = devices // 2
    me = lax.axis_index("date")
    side = me // half
    lane = me % BAND
    rows, columns = images.shape[2:]
    blocks = columns // LANES
    pairs = pair_list.shape[0]
    tiles = half // SUB
    assert images.shape[0] == 1 and rows == SUB * half and half % SUB == 0
    assert columns == blocks * LANES == LANES * LOOK_COLS and blocks % BOX_PARTS == 0
    vmem = pl.BlockSpec(memory_space=pltpu.VMEM)
    smem = pl.BlockSpec(memory_space=pltpu.SMEM)
    place = jnp.stack([side, lane]).astype(jnp.int32)

    beside = lax.ppermute(height_phase, "date", [(k, k ^ 1) for k in range(devices)])

    packed = jnp.swapaxes(images[0].reshape(2, half, SUB, columns), 0, 1)
    packed = packed.reshape(half, 2 * SUB, columns)
    edges = pl.pallas_call(
        functools.partial(edge_kernel, half),
        out_shape=[jax.ShapeDtypeStruct((2 * SUB, columns), jnp.float32)] * (half // 2),
        in_specs=[pl.BlockSpec(memory_space=pltpu.HBM)],
        out_specs=[vmem] * (half // 2),
        scratch_shapes=[pltpu.SemaphoreType.DMA((half // 2,))],
        name="edge_lines",
    )(packed)
    halves = [list(range(half)), list(range(half, devices))]
    own = lax.all_to_all(
        packed, "date", split_axis=0, concat_axis=0, tiled=True, axis_index_groups=halves
    )

    def as_rows(values):
        values = values.reshape(-1, SUB, blocks, LANES)
        return jnp.swapaxes(values, 1, 2).reshape(-1, LANES)

    halos = []
    for i in range(BAND):
        arrived = None
        for g in range(half // 2 // BAND):
            steps = []
            for a in range(BAND):
                steps.append((half + a, half // 2 + BAND * g + (a ^ i)))
                steps.append((half - BAND + a, half + BAND * g + (a ^ i)))
            got = lax.ppermute(edges[BAND * g + i], "date", steps)
            arrived = got if arrived is None else arrived + got
        halos.append(as_rows(arrived))

    low = side == 0
    both = jnp.where(
        me % 2 == 0,
        jnp.concatenate([height_phase, beside]),
        jnp.concatenate([beside, height_phase]),
    )
    phase = lax.ppermute(
        both, "date", [(k, k // 2 + k % 2 * half) for k in range(devices)]
    )
    own_factors = lax.dynamic_slice_in_dim(baseline, side * half, half)
    edge_factors = lax.dynamic_slice_in_dim(
        baseline, jnp.where(low, half, half - BAND), BAND
    )
    factors = 0.5 * jnp.concatenate([own_factors, edge_factors, edge_factors])
    factors = jnp.broadcast_to(factors[:, None], (half + SUB, LANES))
    sums = ((1 + 2 * BAND) * tiles + 1) * ROW_SETS * SUB
    slot_rows = devices * CAP * SLOT_ROWS
    owners = pair_owner[:, 0]
    first = pair_list[:, 0]
    second = pair_list[:, 1]
    earlier = jnp.tril(owners[:, None] == owners[None, :], -1)
    slot = owners * CAP + jnp.sum(earlier.astype(jnp.int32), axis=1)
    held = (second - first - 1) * half + jnp.where(low, first, second - half)
    held = jnp.where(jnp.where(low, first < half, second >= half), held, BAND * half)
    buffer = pl.pallas_call(
        functools.partial(pair_kernel, half, blocks, pairs),
        out_shape=jax.ShapeDtypeStruct((slot_rows, LANES), jnp.float32),
        in_specs=[smem] + [vmem] * (BAND + 3),
        out_specs=vmem,
        scratch_shapes=[
            pltpu.VMEM((2, SUB * BAND, LANES), jnp.float32),
            pltpu.VMEM((sums, columns), jnp.float32),
            pltpu.VMEM((columns // BOX_PARTS, LANES), jnp.bfloat16),
            pltpu.VMEM((BAND * half * SUB + SUB, LANES), jnp.float32),
        ],
        compiler_params=pltpu.CompilerParams(vmem_limit_bytes=(12 + 12 * tiles) * MIB),
        name="pair_products",
    )(
        jnp.concatenate([place, slot, held]),
        factors,
        phase,
        as_rows(own.reshape(half * 2, SUB, columns)),
        *halos,
    )
    delivered = lax.all_to_all(
        buffer.reshape(devices, CAP * SLOT_ROWS, LANES),
        "date",
        split_axis=0,
        concat_axis=0,
        tiled=True,
    )
    look_rows = rows // LOOK_ROWS
    return pl.pallas_call(
        functools.partial(collect_kernel, half),
        out_shape=(
            jax.ShapeDtypeStruct((CAP, 2, look_rows, LANES), jnp.float32),
            jax.ShapeDtypeStruct((CAP, look_rows, LANES), jnp.float32),
        ),
        in_specs=[vmem],
        out_specs=(vmem, vmem),
        compiler_params=pltpu.CompilerParams(vmem_limit_bytes=16 * MIB),
        name="collect_slots",
    )(delivered.reshape(slot_rows, LANES))


def solution(mesh):
    in_specs = (
        P(("groups", "date"), None, None, None),
        P(("groups", "date"), None),
        P("groups"),
        P(),
        P(),
    )
    out_specs = (P(("groups", "date"), None, None, None), P(("groups", "date"), None, None))
    return jax.shard_map(body, mesh=mesh, in_specs=in_specs, out_specs=out_specs, check_vma=False)
```

```python
import functools

import jax
import jax.numpy as jnp
from jax import lax
from jax.experimental import pallas as pl
from jax.experimental.pallas import tpu as pltpu
from jax.sharding import PartitionSpec as P

LOOK_ROWS = 4
LOOK_COLS = 20
BAND = 4
CAP = 4
EPSILON = 1e-06

LANES = 128
SUB = 8
ROW_SETS = SUB // LOOK_ROWS
KINDS = 3
SLOT_ROWS = KINDS * ROW_SETS
BOX_PARTS = 4
MIB = 1024 * 1024


SINE = (1.0, -0.1666666567325592, 0.00833327230066061, -0.00019829686789307743, 2.665147349034669e-06)
COSINE = (1.0, -0.49999988079071045, 0.041666001081466675, -0.001387619529850781, 2.3807961042621173e-05)


def cosine_and_sine(x):
    z = x * x
    s = SINE[-1]
    for c in SINE[-2::-1]:
        s = s * z + c
    s = s * x
    c = COSINE[-1]
    for d in COSINE[-2::-1]:
        c = c * z + d
    twice = s + s
    return 1.0 - twice * s, twice * c


def edge_kernel(half, packed_ref, *rest):
    edge_refs = rest[: half // 2]
    sem = rest[half // 2]
    me = lax.axis_index("date")
    lane = lax.rem(me, BAND)
    first = jnp.where(me < half, 0, half // 2)
    arriving = []
    for n, edge_ref in enumerate(edge_refs):
        target = first + n // BAND * BAND + jnp.bitwise_xor(lane, n % BAND)
        arriving.append(
            pltpu.make_async_copy(packed_ref.at[target], edge_ref, sem.at[n])
        )
        arriving[-1].start()
    for copy in arriving:
        copy.wait()


def pair_kernel(half, blocks, pairs, place_ref, factor_ref, phase_ref, own_ref, *rest):
    halo_refs = rest[:BAND]
    out_ref, raw_ref, sum_ref, box_ref, result_ref = rest[BAND:]
    tiles = half // SUB
    per_part = blocks * SUB
    per_date = 2 * per_part
    side = place_ref[0]
    lane = place_ref[1]
    low = side == 0
    row_index = lax.broadcasted_iota(jnp.int32, (SUB, LANES), 0)
    masks = []
    shifts = []
    for k in range(1, BAND + 1):
        masks.append(
            jnp.where(low, row_index - k, SUB - 1 - k - row_index) >= 0
        )
        shifts.append(jnp.where(low, SUB - k, k))

    def partners(values, edge):
        found = []
        for tile in range(tiles):
            after = values[tile + 1] if tile + 1 < tiles else edge
            before = values[tile - 1] if tile > 0 else edge
            beside = edge if tiles == 1 else jnp.where(low, after, before)
            found.append(
                [
                    pltpu.roll(jnp.where(masks[k], values[tile], beside), shifts[k], 0)
                    for k in range(BAND)
                ]
            )
        return found

    box_columns = box_ref.shape[0]
    offset = lax.broadcasted_iota(
        jnp.int32, (box_columns, LANES), 0
    ) - LOOK_COLS * lax.broadcasted_iota(jnp.int32, (box_columns, LANES), 1)
    inside = jnp.where((offset >= 0) & (offset < LOOK_COLS), 1.0, 0.0)
    box_ref[...] = inside.astype(jnp.bfloat16)

    def turned(angle, real, imag):
        cosine, sine_part = cosine_and_sine(angle)
        return real * cosine - imag * sine_part, real * sine_part + imag * cosine

    first_row = row_index < BAND
    to_even = SUB // 2 * side
    to_odd = SUB // 2 - to_even
    edge_kind = 1 + 2 * BAND

    def block(t, carry):
        line_at = pl.multiple_of(t * SUB, SUB)
        column = pl.ds(pl.multiple_of(t * LANES, LANES), LANES)
        for part in range(2):
            for i in range(BAND):
                row = jnp.bitwise_xor(lane, i)
                raw_ref[part, pl.ds(row, SUB, stride=BAND), :] = halo_refs[i][
                    pl.ds(part * per_part + line_at, SUB), :
                ]
        for b in range(ROW_SETS):
            sums = {}

            def add(key, term):
                sums[key] = sums[key] + term if key in sums else term

            for even in range(b * LOOK_ROWS, (b + 1) * LOOK_ROWS, 2):
                phases = [phase_ref[line : line + 1, column] for line in (even, even + 1)]
                span = slice(even * BAND, even * BAND + SUB)
                edge = turned(
                    factor_ref[tiles * SUB :, :] * jnp.where(first_row, *phases),
                    raw_ref[0, span, :],
                    raw_ref[1, span, :],
                )
                add((edge_kind, 0), edge[0] * edge[0] + edge[1] * edge[1])
                for line in (even, even + 1):
                    to_place = to_even if line == even else to_odd
                    edge_real, edge_imag = [pltpu.roll(v, to_place, 0) for v in edge]
                    reals = []
                    imags = []
                    for tile in range(tiles):
                        start = tile * SUB * per_date + line_at + line
                        real, imag = turned(
                            factor_ref[tile * SUB : (tile + 1) * SUB, :]
                            * phases[line - even],
                            own_ref[pl.ds(start, SUB, stride=per_date), :],
                            own_ref[pl.ds(start + per_part, SUB, stride=per_date), :],
                        )
                        add((0, tile), real * real + imag * imag)
                        reals.append(real)
                        imags.append(imag)
                    other_reals = partners(reals, edge_real)
                    other_imags = partners(imags, edge_imag)
                    for tile in range(tiles):
                        for k in range(BAND):
                            other_real = other_reals[tile][k]
                            other_imag = other_imags[tile][k]
                            real = reals[tile]
                            imag = imags[tile]
                            add((1 + 2 * k, tile), real * other_real + imag * other_imag)
                            add((2 + 2 * k, tile), imag * other_real - real * other_imag)
            for (kind, tile), value in sums.items():
                at = sum_row(kind, b, tile)
                sum_ref[at : at + SUB, column] = value
        return carry

    def sum_row(kind, b, tile):
        return (kind * tiles * ROW_SETS + b * (1 if kind == edge_kind else tiles) + tile) * SUB

    lax.fori_loop(0, blocks, block, 0, unroll=4 if tiles == 1 else 1)

    box = box_ref[...]
    looked = None
    for part in range(sum_ref.shape[1] // box_columns):
        rest_of = sum_ref[:, part * box_columns : (part + 1) * box_columns]
        parts = None
        for piece in range(2):
            rounded = rest_of.astype(jnp.bfloat16)
            value = jnp.dot(rounded, box, preferred_element_type=jnp.float32)
            parts = value if parts is None else parts + value
            if piece < 1:
                rest_of = rest_of - rounded.astype(jnp.float32)
        if part:
            parts = pltpu.roll(parts, part * (box_columns // LOOK_COLS), 1)
        looked = parts if looked is None else looked + parts
    looked = looked * (1.0 / (LOOK_ROWS * LOOK_COLS))

    def rows_of(kind, b, tile):
        at = sum_row(kind, b, tile)
        return looked[at : at + SUB, :]

    sign = jnp.where(low, 1.0, -1.0)
    for b in range(ROW_SETS):
        powers = [rows_of(0, b, tile) for tile in range(tiles)]
        edge_power = rows_of(edge_kind, b, 0)
        other_powers = partners(powers, edge_power + pltpu.roll(edge_power, SUB // 2, 0))
        for tile in range(tiles):
            for k in range(BAND):
                look_real = rows_of(1 + 2 * k, b, tile)
                look_imag = rows_of(2 + 2 * k, b, tile) * sign
                coherence = jnp.sqrt(
                    look_real * look_real + look_imag * look_imag
                ) / jnp.sqrt((powers[tile] + EPSILON) * (other_powers[tile][k] + EPSILON))
                for kind, value in enumerate((look_real, look_imag, coherence)):
                    at = (k * half + tile * SUB) * SUB + kind * ROW_SETS + b
                    result_ref[pl.ds(at, SUB, stride=SUB), :] = value

    out_ref[...] = jnp.zeros_like(out_ref)
    result_ref[BAND * half * SUB :, :] = jnp.zeros((SUB, LANES), jnp.float32)
    for p in range(pairs):
        taken = pl.multiple_of(place_ref[2 + pairs + p] * SUB, SUB)
        out_ref[pl.ds(place_ref[2 + p] * SLOT_ROWS, SLOT_ROWS), :] = result_ref[
            pl.ds(taken, SUB), :
        ][:SLOT_ROWS]


def collect_kernel(half, got_ref, look_ref, coherence_ref):
    per_device = CAP * SLOT_ROWS
    for tile in range(half // SUB):
        for slot in range(CAP):
            for kind in range(KINDS):
                for b in range(ROW_SETS):
                    at = tile * SUB * per_device + slot * SLOT_ROWS + kind * ROW_SETS + b
                    value = got_ref[pl.ds(at, SUB, stride=per_device), :]
                    at += half * per_device
                    value += got_ref[pl.ds(at, SUB, stride=per_device), :]
                    spot = pl.ds(tile * SUB * ROW_SETS + b, SUB, stride=ROW_SETS)
                    if kind < 2:
                        look_ref[slot, kind, spot, :] = value
                    else:
                        coherence_ref[slot, spot, :] = value


def body(images, height_phase, baseline, pair_list, pair_owner):
    devices = lax.axis_size("date")
    half = devices // 2
    me = lax.axis_index("date")
    side = me // half
    lane = me % BAND
    rows, columns = images.shape[2:]
    blocks = columns // LANES
    pairs = pair_list.shape[0]
    tiles = half // SUB
    assert images.shape[0] == 1 and rows == SUB * half and half % SUB == 0
    assert columns == blocks * LANES == LANES * LOOK_COLS and blocks % BOX_PARTS == 0
    vmem = pl.BlockSpec(memory_space=pltpu.VMEM)
    smem = pl.BlockSpec(memory_space=pltpu.SMEM)
    place = jnp.stack([side, lane]).astype(jnp.int32)

    beside = lax.ppermute(height_phase, "date", [(k, k ^ 1) for k in range(devices)])

    packed = jnp.swapaxes(images[0].reshape(2, half, SUB, columns), 0, 1)
    packed = packed.reshape(half, 2 * SUB, columns)
    edges = pl.pallas_call(
        functools.partial(edge_kernel, half),
        out_shape=[jax.ShapeDtypeStruct((2 * SUB, columns), jnp.float32)] * (half // 2),
        in_specs=[pl.BlockSpec(memory_space=pltpu.HBM)],
        out_specs=[vmem] * (half // 2),
        scratch_shapes=[pltpu.SemaphoreType.DMA((half // 2,))],
        name="edge_lines",
    )(packed)
    halves = [list(range(half)), list(range(half, devices))]
    own = lax.all_to_all(
        packed, "date", split_axis=0, concat_axis=0, tiled=True, axis_index_groups=halves
    )

    def as_rows(values):
        values = values.reshape(-1, SUB, blocks, LANES)
        return jnp.swapaxes(values, 1, 2).reshape(-1, LANES)

    halos = []
    for i in range(BAND):
        arrived = None
        for g in range(half // 2 // BAND):
            steps = []
            for a in range(BAND):
                steps.append((half + a, half // 2 + BAND * g + (a ^ i)))
                steps.append((half - BAND + a, half + BAND * g + (a ^ i)))
            got = lax.ppermute(edges[BAND * g + i], "date", steps)
            arrived = got if arrived is None else arrived + got
        halos.append(as_rows(arrived))

    low = side == 0
    both = jnp.where(
        me % 2 == 0,
        jnp.concatenate([height_phase, beside]),
        jnp.concatenate([beside, height_phase]),
    )
    phase = lax.ppermute(
        both, "date", [(k, k // 2 + k % 2 * half) for k in range(devices)]
    )
    own_factors = lax.dynamic_slice_in_dim(baseline, side * half, half)
    edge_factors = lax.dynamic_slice_in_dim(
        baseline, jnp.where(low, half, half - BAND), BAND
    )
    factors = 0.5 * jnp.concatenate([own_factors, edge_factors, edge_factors])
    factors = jnp.broadcast_to(factors[:, None], (half + SUB, LANES))
    sums = ((1 + 2 * BAND) * tiles + 1) * ROW_SETS * SUB
    slot_rows = devices * CAP * SLOT_ROWS
    owners = pair_owner[:, 0]
    first = pair_list[:, 0]
    second = pair_list[:, 1]
    earlier = jnp.tril(owners[:, None] == owners[None, :], -1)
    slot = owners * CAP + jnp.sum(earlier.astype(jnp.int32), axis=1)
    held = (second - first - 1) * half + jnp.where(low, first, second - half)
    held = jnp.where(jnp.where(low, first < half, second >= half), held, BAND * half)
    buffer = pl.pallas_call(
        functools.partial(pair_kernel, half, blocks, pairs),
        out_shape=jax.ShapeDtypeStruct((slot_rows, LANES), jnp.float32),
        in_specs=[smem] + [vmem] * (BAND + 3),
        out_specs=vmem,
        scratch_shapes=[
            pltpu.VMEM((2, SUB * BAND, LANES), jnp.float32),
            pltpu.VMEM((sums, columns), jnp.float32),
            pltpu.VMEM((columns // BOX_PARTS, LANES), jnp.bfloat16),
            pltpu.VMEM((BAND * half * SUB + SUB, LANES), jnp.float32),
        ],
        compiler_params=pltpu.CompilerParams(vmem_limit_bytes=(12 + 12 * tiles) * MIB),
        name="pair_products",
    )(
        jnp.concatenate([place, slot, held]),
        factors,
        phase,
        as_rows(own.reshape(half * 2, SUB, columns)),
        *halos,
    )
    delivered = lax.all_to_all(
        buffer.reshape(devices, CAP * SLOT_ROWS, LANES),
        "date",
        split_axis=0,
        concat_axis=0,
        tiled=True,
    )
    look_rows = rows // LOOK_ROWS
    return pl.pallas_call(
        functools.partial(collect_kernel, half),
        out_shape=(
            jax.ShapeDtypeStruct((CAP, 2, look_rows, LANES), jnp.float32),
            jax.ShapeDtypeStruct((CAP, look_rows, LANES), jnp.float32),
        ),
        in_specs=[vmem],
        out_specs=(vmem, vmem),
        compiler_params=pltpu.CompilerParams(vmem_limit_bytes=16 * MIB),
        name="collect_slots",
    )(delivered.reshape(slot_rows, LANES))


def solution(mesh):
    in_specs = (
        P(("groups", "date"), None, None, None),
        P(("groups", "date"), None),
        P("groups"),
        P(),
        P(),
    )
    out_specs = (P(("groups", "date"), None, None, None), P(("groups", "date"), None, None))
    return jax.shard_map(body, mesh=mesh, in_specs=in_specs, out_specs=out_specs, check_vma=False)
```

```python
import functools

import jax
import jax.numpy as jnp
from jax import lax
from jax.experimental import pallas as pl
from jax.experimental.pallas import tpu as pltpu
from jax.sharding import PartitionSpec as P

LOOK_ROWS = 4
LOOK_COLS = 20
BAND = 4
CAP = 4
EPSILON = 1e-06

LANES = 128
SUB = 8
ROW_SETS = SUB // LOOK_ROWS
KINDS = 3
SLOT_ROWS = KINDS * ROW_SETS
BOX_PARTS = 4
MIB = 1024 * 1024


SINE = (1.0, -0.1666666567325592, 0.00833327230066061, -0.00019829686789307743, 2.665147349034669e-06)
COSINE = (1.0, -0.49999988079071045, 0.041666001081466675, -0.001387619529850781, 2.3807961042621173e-05)


def cosine_and_sine(x):
    z = x * x
    s = SINE[-1]
    for c in SINE[-2::-1]:
        s = s * z + c
    s = s * x
    c = COSINE[-1]
    for d in COSINE[-2::-1]:
        c = c * z + d
    twice = s + s
    return 1.0 - twice * s, twice * c


def edge_kernel(half, packed_ref, *rest):
    edge_refs = rest[: half // 2]
    sem = rest[half // 2]
    me = lax.axis_index("date")
    lane = lax.rem(me, BAND)
    first = jnp.where(me < half, 0, half // 2)
    arriving = []
    for n, edge_ref in enumerate(edge_refs):
        target = first + n // BAND * BAND + jnp.bitwise_xor(lane, n % BAND)
        arriving.append(
            pltpu.make_async_copy(packed_ref.at[target], edge_ref, sem.at[n])
        )
        arriving[-1].start()
    for copy in arriving:
        copy.wait()


def pair_kernel(half, blocks, pairs, place_ref, factor_ref, phase_ref, own_ref, *rest):
    halo_refs = rest[:BAND]
    out_ref, raw_ref, sum_ref, box_ref, result_ref = rest[BAND:]
    tiles = half // SUB
    per_part = blocks * SUB
    per_date = 2 * per_part
    side = place_ref[0]
    lane = place_ref[1]
    low = side == 0
    row_index = lax.broadcasted_iota(jnp.int32, (SUB, LANES), 0)
    masks = []
    shifts = []
    for k in range(1, BAND + 1):
        masks.append(
            jnp.where(low, row_index - k, SUB - 1 - k - row_index) >= 0
        )
        shifts.append(jnp.where(low, SUB - k, k))

    def partners(values, edge):
        found = []
        for tile in range(tiles):
            after = values[tile + 1] if tile + 1 < tiles else edge
            before = values[tile - 1] if tile > 0 else edge
            beside = edge if tiles == 1 else jnp.where(low, after, before)
            found.append(
                [
                    pltpu.roll(jnp.where(masks[k], values[tile], beside), shifts[k], 0)
                    for k in range(BAND)
                ]
            )
        return found

    box_columns = box_ref.shape[0]
    offset = lax.broadcasted_iota(
        jnp.int32, (box_columns, LANES), 0
    ) - LOOK_COLS * lax.broadcasted_iota(jnp.int32, (box_columns, LANES), 1)
    inside = jnp.where((offset >= 0) & (offset < LOOK_COLS), 1.0, 0.0)
    box_ref[...] = inside.astype(jnp.bfloat16)

    def turned(angle, real, imag):
        cosine, sine_part = cosine_and_sine(angle)
        return real * cosine - imag * sine_part, real * sine_part + imag * cosine

    first_row = row_index < BAND
    to_even = SUB // 2 * side
    to_odd = SUB // 2 - to_even
    edge_kind = 1 + 2 * BAND

    def block(t, carry):
        line_at = t * SUB
        column = pl.ds(t * LANES, LANES)
        if not isinstance(t, int):
            line_at = pl.multiple_of(line_at, SUB)
            column = pl.ds(pl.multiple_of(t * LANES, LANES), LANES)
        for part in range(2):
            for i in range(BAND):
                row = jnp.bitwise_xor(lane, i)
                raw_ref[part, pl.ds(row, SUB, stride=BAND), :] = halo_refs[i][
                    pl.ds(part * per_part + line_at, SUB), :
                ]
        for b in range(ROW_SETS):
            sums = {}

            def add(key, term):
                sums[key] = sums[key] + term if key in sums else term

            for even in range(b * LOOK_ROWS, (b + 1) * LOOK_ROWS, 2):
                phases = [phase_ref[line : line + 1, column] for line in (even, even + 1)]
                span = slice(even * BAND, even * BAND + SUB)
                edge = turned(
                    factor_ref[tiles * SUB :, :] * jnp.where(first_row, *phases),
                    raw_ref[0, span, :],
                    raw_ref[1, span, :],
                )
                add((edge_kind, 0), edge[0] * edge[0] + edge[1] * edge[1])
                for line in (even, even + 1):
                    to_place = to_even if line == even else to_odd
                    edge_real, edge_imag = [pltpu.roll(v, to_place, 0) for v in edge]
                    reals = []
                    imags = []
                    for tile in range(tiles):
                        start = tile * SUB * per_date + line_at + line
                        real, imag = turned(
                            factor_ref[tile * SUB : (tile + 1) * SUB, :]
                            * phases[line - even],
                            own_ref[pl.ds(start, SUB, stride=per_date), :],
                            own_ref[pl.ds(start + per_part, SUB, stride=per_date), :],
                        )
                        add((0, tile), real * real + imag * imag)
                        reals.append(real)
                        imags.append(imag)
                    other_reals = partners(reals, edge_real)
                    other_imags = partners(imags, edge_imag)
                    for tile in range(tiles):
                        for k in range(BAND):
                            other_real = other_reals[tile][k]
                            other_imag = other_imags[tile][k]
                            real = reals[tile]
                            imag = imags[tile]
                            add((1 + 2 * k, tile), real * other_real + imag * other_imag)
                            add((2 + 2 * k, tile), imag * other_real - real * other_imag)
            for (kind, tile), value in sums.items():
                at = sum_row(kind, b, tile)
                sum_ref[at : at + SUB, column] = value
        return carry

    def sum_row(kind, b, tile):
        return (kind * tiles * ROW_SETS + b * (1 if kind == edge_kind else tiles) + tile) * SUB

    box = box_ref[...]
    looked = None
    for part in range(BOX_PARTS):
        first = part * (blocks // BOX_PARTS)
        last = first + blocks // BOX_PARTS
        if tiles == 1:
            for t in range(first, last):
                block(t, 0)
        else:
            lax.fori_loop(first, last, block, 0)
        rest_of = sum_ref[:, part * box_columns : (part + 1) * box_columns]
        parts = None
        for piece in range(2):
            rounded = rest_of.astype(jnp.bfloat16)
            value = jnp.dot(rounded, box, preferred_element_type=jnp.float32)
            parts = value if parts is None else parts + value
            if piece < 1:
                rest_of = rest_of - rounded.astype(jnp.float32)
        if part:
            parts = pltpu.roll(parts, part * (box_columns // LOOK_COLS), 1)
        looked = parts if looked is None else looked + parts
    looked = looked * (1.0 / (LOOK_ROWS * LOOK_COLS))

    def rows_of(kind, b, tile):
        at = sum_row(kind, b, tile)
        return looked[at : at + SUB, :]

    sign = jnp.where(low, 1.0, -1.0)
    for b in range(ROW_SETS):
        powers = [rows_of(0, b, tile) for tile in range(tiles)]
        edge_power = rows_of(edge_kind, b, 0)
        other_powers = partners(powers, edge_power + pltpu.roll(edge_power, SUB // 2, 0))
        for tile in range(tiles):
            for k in range(BAND):
                look_real = rows_of(1 + 2 * k, b, tile)
                look_imag = rows_of(2 + 2 * k, b, tile) * sign
                coherence = jnp.sqrt(
                    look_real * look_real + look_imag * look_imag
                ) / jnp.sqrt((powers[tile] + EPSILON) * (other_powers[tile][k] + EPSILON))
                for kind, value in enumerate((look_real, look_imag, coherence)):
                    at = (k * half + tile * SUB) * SUB + kind * ROW_SETS + b
                    result_ref[pl.ds(at, SUB, stride=SUB), :] = value

    out_ref[...] = jnp.zeros_like(out_ref)
    result_ref[BAND * half * SUB :, :] = jnp.zeros((SUB, LANES), jnp.float32)
    for p in range(pairs):
        taken = pl.multiple_of(place_ref[2 + pairs + p] * SUB, SUB)
        out_ref[pl.ds(place_ref[2 + p] * SLOT_ROWS, SLOT_ROWS), :] = result_ref[
            pl.ds(taken, SUB), :
        ][:SLOT_ROWS]


def collect_kernel(half, got_ref, look_ref, coherence_ref):
    per_device = CAP * SLOT_ROWS
    for tile in range(half // SUB):
        for slot in range(CAP):
            for kind in range(KINDS):
                for b in range(ROW_SETS):
                    at = tile * SUB * per_device + slot * SLOT_ROWS + kind * ROW_SETS + b
                    value = got_ref[pl.ds(at, SUB, stride=per_device), :]
                    at += half * per_device
                    value += got_ref[pl.ds(at, SUB, stride=per_device), :]
                    spot = pl.ds(tile * SUB * ROW_SETS + b, SUB, stride=ROW_SETS)
                    if kind < 2:
                        look_ref[slot, kind, spot, :] = value
                    else:
                        coherence_ref[slot, spot, :] = value


def body(images, height_phase, baseline, pair_list, pair_owner):
    devices = lax.axis_size("date")
    half = devices // 2
    me = lax.axis_index("date")
    side = me // half
    lane = me % BAND
    rows, columns = images.shape[2:]
    blocks = columns // LANES
    pairs = pair_list.shape[0]
    tiles = half // SUB
    assert images.shape[0] == 1 and rows == SUB * half and half % SUB == 0
    assert columns == blocks * LANES == LANES * LOOK_COLS and blocks % BOX_PARTS == 0
    vmem = pl.BlockSpec(memory_space=pltpu.VMEM)
    smem = pl.BlockSpec(memory_space=pltpu.SMEM)
    place = jnp.stack([side, lane]).astype(jnp.int32)

    beside = lax.ppermute(height_phase, "date", [(k, k ^ 1) for k in range(devices)])

    packed = jnp.swapaxes(images[0].reshape(2, half, SUB, columns), 0, 1)
    packed = packed.reshape(half, 2 * SUB, columns)
    edges = pl.pallas_call(
        functools.partial(edge_kernel, half),
        out_shape=[jax.ShapeDtypeStruct((2 * SUB, columns), jnp.float32)] * (half // 2),
        in_specs=[pl.BlockSpec(memory_space=pltpu.HBM)],
        out_specs=[vmem] * (half // 2),
        scratch_shapes=[pltpu.SemaphoreType.DMA((half // 2,))],
        name="edge_lines",
    )(packed)
    halves = [list(range(half)), list(range(half, devices))]
    own = lax.all_to_all(
        packed, "date", split_axis=0, concat_axis=0, tiled=True, axis_index_groups=halves
    )

    def as_rows(values):
        values = values.reshape(-1, SUB, blocks, LANES)
        return jnp.swapaxes(values, 1, 2).reshape(-1, LANES)

    halos = []
    for i in range(BAND):
        arrived = None
        for g in range(half // 2 // BAND):
            steps = []
            for a in range(BAND):
                steps.append((half + a, half // 2 + BAND * g + (a ^ i)))
                steps.append((half - BAND + a, half + BAND * g + (a ^ i)))
            got = lax.ppermute(edges[BAND * g + i], "date", steps)
            arrived = got if arrived is None else arrived + got
        halos.append(as_rows(arrived))

    low = side == 0
    both = jnp.where(
        me % 2 == 0,
        jnp.concatenate([height_phase, beside]),
        jnp.concatenate([beside, height_phase]),
    )
    phase = lax.ppermute(
        both, "date", [(k, k // 2 + k % 2 * half) for k in range(devices)]
    )
    own_factors = lax.dynamic_slice_in_dim(baseline, side * half, half)
    edge_factors = lax.dynamic_slice_in_dim(
        baseline, jnp.where(low, half, half - BAND), BAND
    )
    factors = 0.5 * jnp.concatenate([own_factors, edge_factors, edge_factors])
    factors = jnp.broadcast_to(factors[:, None], (half + SUB, LANES))
    sums = ((1 + 2 * BAND) * tiles + 1) * ROW_SETS * SUB
    slot_rows = devices * CAP * SLOT_ROWS
    owners = pair_owner[:, 0]
    first = pair_list[:, 0]
    second = pair_list[:, 1]
    earlier = jnp.tril(owners[:, None] == owners[None, :], -1)
    slot = owners * CAP + jnp.sum(earlier.astype(jnp.int32), axis=1)
    held = (second - first - 1) * half + jnp.where(low, first, second - half)
    held = jnp.where(jnp.where(low, first < half, second >= half), held, BAND * half)
    buffer = pl.pallas_call(
        functools.partial(pair_kernel, half, blocks, pairs),
        out_shape=jax.ShapeDtypeStruct((slot_rows, LANES), jnp.float32),
        in_specs=[smem] + [vmem] * (BAND + 3),
        out_specs=vmem,
        scratch_shapes=[
            pltpu.VMEM((2, SUB * BAND, LANES), jnp.float32),
            pltpu.VMEM((sums, columns), jnp.float32),
            pltpu.VMEM((columns // BOX_PARTS, LANES), jnp.bfloat16),
            pltpu.VMEM((BAND * half * SUB + SUB, LANES), jnp.float32),
        ],
        compiler_params=pltpu.CompilerParams(vmem_limit_bytes=(12 + 12 * tiles) * MIB),
        name="pair_products",
    )(
        jnp.concatenate([place, slot, held]),
        factors,
        phase,
        as_rows(own.reshape(half * 2, SUB, columns)),
        *halos,
    )
    delivered = lax.all_to_all(
        buffer.reshape(devices, CAP * SLOT_ROWS, LANES),
        "date",
        split_axis=0,
        concat_axis=0,
        tiled=True,
    )
    look_rows = rows // LOOK_ROWS
    return pl.pallas_call(
        functools.partial(collect_kernel, half),
        out_shape=(
            jax.ShapeDtypeStruct((CAP, 2, look_rows, LANES), jnp.float32),
            jax.ShapeDtypeStruct((CAP, look_rows, LANES), jnp.float32),
        ),
        in_specs=[vmem],
        out_specs=(vmem, vmem),
        compiler_params=pltpu.CompilerParams(vmem_limit_bytes=16 * MIB),
        name="collect_slots",
    )(delivered.reshape(slot_rows, LANES))


def solution(mesh):
    in_specs = (
        P(("groups", "date"), None, None, None),
        P(("groups", "date"), None),
        P("groups"),
        P(),
        P(),
    )
    out_specs = (P(("groups", "date"), None, None, None), P(("groups", "date"), None, None))
    return jax.shard_map(body, mesh=mesh, in_specs=in_specs, out_specs=out_specs, check_vma=False)
```

```python
import functools

import jax
import jax.numpy as jnp
from jax import lax
from jax.experimental import pallas as pl
from jax.experimental.pallas import tpu as pltpu
from jax.sharding import PartitionSpec as P

LOOK_ROWS = 4
LOOK_COLS = 20
BAND = 4
CAP = 4
EPSILON = 1e-06

LANES = 128
SUB = 8
ROW_SETS = SUB // LOOK_ROWS
KINDS = 3
SLOT_ROWS = KINDS * ROW_SETS
BOX_PARTS = 4
MIB = 1024 * 1024


SINE = (1.0, -0.1666666567325592, 0.00833327230066061, -0.00019829686789307743, 2.665147349034669e-06)
COSINE = (1.0, -0.49999988079071045, 0.041666001081466675, -0.001387619529850781, 2.3807961042621173e-05)


def cosine_and_sine(x):
    z = x * x
    s = SINE[-1]
    for c in SINE[-2::-1]:
        s = s * z + c
    s = s * x
    c = COSINE[-1]
    for d in COSINE[-2::-1]:
        c = c * z + d
    twice = s + s
    return 1.0 - twice * s, twice * c


def edge_kernel(half, n, packed_ref, edge_ref, sem):
    me = lax.axis_index("date")
    first = jnp.where(me < half, 0, half // 2)
    target = first + n // BAND * BAND + jnp.bitwise_xor(lax.rem(me, BAND), n % BAND)
    copy = pltpu.make_async_copy(packed_ref.at[target], edge_ref, sem)
    copy.start()
    copy.wait()


def pair_kernel(half, blocks, pairs, place_ref, factor_ref, phase_ref, own_ref, *rest):
    halo_refs = rest[:BAND]
    out_ref, raw_ref, sum_ref, box_ref, result_ref = rest[BAND:]
    tiles = half // SUB
    per_part = blocks * SUB
    per_date = 2 * per_part
    side = place_ref[0]
    lane = place_ref[1]
    low = side == 0
    row_index = lax.broadcasted_iota(jnp.int32, (SUB, LANES), 0)
    masks = []
    shifts = []
    for k in range(1, BAND + 1):
        masks.append(
            jnp.where(low, row_index - k, SUB - 1 - k - row_index) >= 0
        )
        shifts.append(jnp.where(low, SUB - k, k))

    def partners(values, edge):
        found = []
        for tile in range(tiles):
            after = values[tile + 1] if tile + 1 < tiles else edge
            before = values[tile - 1] if tile > 0 else edge
            beside = edge if tiles == 1 else jnp.where(low, after, before)
            found.append(
                [
                    pltpu.roll(jnp.where(masks[k], values[tile], beside), shifts[k], 0)
                    for k in range(BAND)
                ]
            )
        return found

    box_columns = box_ref.shape[0]
    offset = lax.broadcasted_iota(
        jnp.int32, (box_columns, LANES), 0
    ) - LOOK_COLS * lax.broadcasted_iota(jnp.int32, (box_columns, LANES), 1)
    inside = jnp.where((offset >= 0) & (offset < LOOK_COLS), 1.0, 0.0)
    box_ref[...] = inside.astype(jnp.bfloat16)

    def turned(angle, real, imag):
        cosine, sine_part = cosine_and_sine(angle)
        return real * cosine - imag * sine_part, real * sine_part + imag * cosine

    first_row = row_index < BAND
    to_even = SUB // 2 * side
    to_odd = SUB // 2 - to_even
    edge_kind = 1 + 2 * BAND

    def block(t, carry):
        line_at = pl.multiple_of(t * SUB, SUB)
        column = pl.ds(pl.multiple_of(t * LANES, LANES), LANES)
        for part in range(2):
            for i in range(BAND):
                row = jnp.bitwise_xor(lane, i)
                raw_ref[part, pl.ds(row, SUB, stride=BAND), :] = halo_refs[i][
                    pl.ds(part * per_part + line_at, SUB), :
                ]
        for b in range(ROW_SETS):
            sums = {}

            def add(key, term):
                sums[key] = sums[key] + term if key in sums else term

            for even in range(b * LOOK_ROWS, (b + 1) * LOOK_ROWS, 2):
                phases = [phase_ref[line : line + 1, column] for line in (even, even + 1)]
                span = slice(even * BAND, even * BAND + SUB)
                edge = turned(
                    factor_ref[tiles * SUB :, :] * jnp.where(first_row, *phases),
                    raw_ref[0, span, :],
                    raw_ref[1, span, :],
                )
                add((edge_kind, 0), edge[0] * edge[0] + edge[1] * edge[1])
                for line in (even, even + 1):
                    to_place = to_even if line == even else to_odd
                    edge_real, edge_imag = [pltpu.roll(v, to_place, 0) for v in edge]
                    reals = []
                    imags = []
                    for tile in range(tiles):
                        start = tile * SUB * per_date + line_at + line
                        real, imag = turned(
                            factor_ref[tile * SUB : (tile + 1) * SUB, :]
                            * phases[line - even],
                            own_ref[pl.ds(start, SUB, stride=per_date), :],
                            own_ref[pl.ds(start + per_part, SUB, stride=per_date), :],
                        )
                        add((0, tile), real * real + imag * imag)
                        reals.append(real)
                        imags.append(imag)
                    other_reals = partners(reals, edge_real)
                    other_imags = partners(imags, edge_imag)
                    for tile in range(tiles):
                        for k in range(BAND):
                            other_real = other_reals[tile][k]
                            other_imag = other_imags[tile][k]
                            real = reals[tile]
                            imag = imags[tile]
                            add((1 + 2 * k, tile), real * other_real + imag * other_imag)
                            add((2 + 2 * k, tile), imag * other_real - real * other_imag)
            for (kind, tile), value in sums.items():
                at = sum_row(kind, b, tile)
                sum_ref[at : at + SUB, column] = value
        return carry

    def sum_row(kind, b, tile):
        return (kind * tiles * ROW_SETS + b * (1 if kind == edge_kind else tiles) + tile) * SUB

    lax.fori_loop(0, blocks, block, 0, unroll=4 if tiles == 1 else 1)

    box = box_ref[...]
    looked = None
    for part in range(sum_ref.shape[1] // box_columns):
        rest_of = sum_ref[:, part * box_columns : (part + 1) * box_columns]
        parts = None
        for piece in range(2):
            rounded = rest_of.astype(jnp.bfloat16)
            value = jnp.dot(rounded, box, preferred_element_type=jnp.float32)
            parts = value if parts is None else parts + value
            if piece < 1:
                rest_of = rest_of - rounded.astype(jnp.float32)
        if part:
            parts = pltpu.roll(parts, part * (box_columns // LOOK_COLS), 1)
        looked = parts if looked is None else looked + parts
    looked = looked * (1.0 / (LOOK_ROWS * LOOK_COLS))

    def rows_of(kind, b, tile):
        at = sum_row(kind, b, tile)
        return looked[at : at + SUB, :]

    sign = jnp.where(low, 1.0, -1.0)
    for b in range(ROW_SETS):
        powers = [rows_of(0, b, tile) for tile in range(tiles)]
        edge_power = rows_of(edge_kind, b, 0)
        other_powers = partners(powers, edge_power + pltpu.roll(edge_power, SUB // 2, 0))
        for tile in range(tiles):
            for k in range(BAND):
                look_real = rows_of(1 + 2 * k, b, tile)
                look_imag = rows_of(2 + 2 * k, b, tile) * sign
                coherence = jnp.sqrt(
                    look_real * look_real + look_imag * look_imag
                ) / jnp.sqrt((powers[tile] + EPSILON) * (other_powers[tile][k] + EPSILON))
                for kind, value in enumerate((look_real, look_imag, coherence)):
                    at = (k * half + tile * SUB) * SUB + kind * ROW_SETS + b
                    result_ref[pl.ds(at, SUB, stride=SUB), :] = value

    out_ref[...] = jnp.zeros_like(out_ref)
    result_ref[BAND * half * SUB :, :] = jnp.zeros((SUB, LANES), jnp.float32)
    for p in range(pairs):
        taken = pl.multiple_of(place_ref[2 + pairs + p] * SUB, SUB)
        out_ref[pl.ds(place_ref[2 + p] * SLOT_ROWS, SLOT_ROWS), :] = result_ref[
            pl.ds(taken, SUB), :
        ][:SLOT_ROWS]


def collect_kernel(half, got_ref, look_ref, coherence_ref):
    per_device = CAP * SLOT_ROWS
    for tile in range(half // SUB):
        for slot in range(CAP):
            for kind in range(KINDS):
                for b in range(ROW_SETS):
                    at = tile * SUB * per_device + slot * SLOT_ROWS + kind * ROW_SETS + b
                    value = got_ref[pl.ds(at, SUB, stride=per_device), :]
                    at += half * per_device
                    value += got_ref[pl.ds(at, SUB, stride=per_device), :]
                    spot = pl.ds(tile * SUB * ROW_SETS + b, SUB, stride=ROW_SETS)
                    if kind < 2:
                        look_ref[slot, kind, spot, :] = value
                    else:
                        coherence_ref[slot, spot, :] = value


def body(images, height_phase, baseline, pair_list, pair_owner):
    devices = lax.axis_size("date")
    half = devices // 2
    me = lax.axis_index("date")
    side = me // half
    lane = me % BAND
    rows, columns = images.shape[2:]
    blocks = columns // LANES
    pairs = pair_list.shape[0]
    tiles = half // SUB
    assert images.shape[0] == 1 and rows == SUB * half and half % SUB == 0
    assert columns == blocks * LANES == LANES * LOOK_COLS and blocks % BOX_PARTS == 0
    vmem = pl.BlockSpec(memory_space=pltpu.VMEM)
    smem = pl.BlockSpec(memory_space=pltpu.SMEM)
    place = jnp.stack([side, lane]).astype(jnp.int32)

    beside = lax.ppermute(height_phase, "date", [(k, k ^ 1) for k in range(devices)])

    packed = jnp.swapaxes(images[0].reshape(2, half, SUB, columns), 0, 1)
    packed = packed.reshape(half, 2 * SUB, columns)
    edges = [
        pl.pallas_call(
            functools.partial(edge_kernel, half, n),
            out_shape=jax.ShapeDtypeStruct((2 * SUB, columns), jnp.float32),
            in_specs=[pl.BlockSpec(memory_space=pltpu.HBM)],
            out_specs=vmem,
            scratch_shapes=[pltpu.SemaphoreType.DMA],
            name="edge_lines",
        )(packed)
        for n in range(half // 2)
    ]
    halves = [list(range(half)), list(range(half, devices))]
    own = lax.all_to_all(
        packed, "date", split_axis=0, concat_axis=0, tiled=True, axis_index_groups=halves
    )

    def as_rows(values):
        values = values.reshape(-1, SUB, blocks, LANES)
        return jnp.swapaxes(values, 1, 2).reshape(-1, LANES)

    halos = []
    for i in range(BAND):
        arrived = None
        for g in range(half // 2 // BAND):
            steps = []
            for a in range(BAND):
                steps.append((half + a, half // 2 + BAND * g + (a ^ i)))
                steps.append((half - BAND + a, half + BAND * g + (a ^ i)))
            got = lax.ppermute(edges[BAND * g + i], "date", steps)
            arrived = got if arrived is None else arrived + got
        halos.append(as_rows(arrived))

    low = side == 0
    both = jnp.where(
        me % 2 == 0,
        jnp.concatenate([height_phase, beside]),
        jnp.concatenate([beside, height_phase]),
    )
    phase = lax.ppermute(
        both, "date", [(k, k // 2 + k % 2 * half) for k in range(devices)]
    )
    own_factors = lax.dynamic_slice_in_dim(baseline, side * half, half)
    edge_factors = lax.dynamic_slice_in_dim(
        baseline, jnp.where(low, half, half - BAND), BAND
    )
    factors = 0.5 * jnp.concatenate([own_factors, edge_factors, edge_factors])
    factors = jnp.broadcast_to(factors[:, None], (half + SUB, LANES))
    sums = ((1 + 2 * BAND) * tiles + 1) * ROW_SETS * SUB
    slot_rows = devices * CAP * SLOT_ROWS
    owners = pair_owner[:, 0]
    first = pair_list[:, 0]
    second = pair_list[:, 1]
    earlier = jnp.tril(owners[:, None] == owners[None, :], -1)
    slot = owners * CAP + jnp.sum(earlier.astype(jnp.int32), axis=1)
    held = (second - first - 1) * half + jnp.where(low, first, second - half)
    held = jnp.where(jnp.where(low, first < half, second >= half), held, BAND * half)
    buffer = pl.pallas_call(
        functools.partial(pair_kernel, half, blocks, pairs),
        out_shape=jax.ShapeDtypeStruct((slot_rows, LANES), jnp.float32),
        in_specs=[smem] + [vmem] * (BAND + 3),
        out_specs=vmem,
        scratch_shapes=[
            pltpu.VMEM((2, SUB * BAND, LANES), jnp.float32),
            pltpu.VMEM((sums, columns), jnp.float32),
            pltpu.VMEM((columns // BOX_PARTS, LANES), jnp.bfloat16),
            pltpu.VMEM((BAND * half * SUB + SUB, LANES), jnp.float32),
        ],
        compiler_params=pltpu.CompilerParams(vmem_limit_bytes=(12 + 12 * tiles) * MIB),
        name="pair_products",
    )(
        jnp.concatenate([place, slot, held]),
        factors,
        phase,
        as_rows(own.reshape(half * 2, SUB, columns)),
        *halos,
    )
    delivered = lax.all_to_all(
        buffer.reshape(devices, CAP * SLOT_ROWS, LANES),
        "date",
        split_axis=0,
        concat_axis=0,
        tiled=True,
    )
    look_rows = rows // LOOK_ROWS
    return pl.pallas_call(
        functools.partial(collect_kernel, half),
        out_shape=(
            jax.ShapeDtypeStruct((CAP, 2, look_rows, LANES), jnp.float32),
            jax.ShapeDtypeStruct((CAP, look_rows, LANES), jnp.float32),
        ),
        in_specs=[vmem],
        out_specs=(vmem, vmem),
        compiler_params=pltpu.CompilerParams(vmem_limit_bytes=16 * MIB),
        name="collect_slots",
    )(delivered.reshape(slot_rows, LANES))


def solution(mesh):
    in_specs = (
        P(("groups", "date"), None, None, None),
        P(("groups", "date"), None),
        P("groups"),
        P(),
        P(),
    )
    out_specs = (P(("groups", "date"), None, None, None), P(("groups", "date"), None, None))
    return jax.shard_map(body, mesh=mesh, in_specs=in_specs, out_specs=out_specs, check_vma=False)
```

```python
import functools

import jax
import jax.numpy as jnp
from jax import lax
from jax.experimental import pallas as pl
from jax.experimental.pallas import tpu as pltpu
from jax.sharding import PartitionSpec as P

LOOK_ROWS = 4
LOOK_COLS = 20
BAND = 4
CAP = 4
EPSILON = 1e-06

LANES = 128
SUB = 8
ROW_SETS = SUB // LOOK_ROWS
KINDS = 3
SLOT_ROWS = KINDS * ROW_SETS
BOX_PARTS = 4
MIB = 1024 * 1024


SINE = (1.0, -0.1666666567325592, 0.00833327230066061, -0.00019829686789307743, 2.665147349034669e-06)
COSINE = (1.0, -0.49999988079071045, 0.041666001081466675, -0.001387619529850781, 2.3807961042621173e-05)


def cosine_and_sine(x):
    z = x * x
    s = SINE[-1]
    for c in SINE[-2::-1]:
        s = s * z + c
    s = s * x
    c = COSINE[-1]
    for d in COSINE[-2::-1]:
        c = c * z + d
    twice = s + s
    return 1.0 - twice * s, twice * c


def edge_kernel(half, packed_ref, *rest):
    edge_refs = rest[: half // 2]
    sem = rest[half // 2]
    me = lax.axis_index("date")
    lane = lax.rem(me, BAND)
    first = jnp.where(me < half, 0, half // 2)
    arriving = []
    for n, edge_ref in enumerate(edge_refs):
        target = first + n // BAND * BAND + jnp.bitwise_xor(lane, n % BAND)
        arriving.append(
            pltpu.make_async_copy(packed_ref.at[target], edge_ref, sem.at[n])
        )
        arriving[-1].start()
    for copy in arriving:
        copy.wait()


def pair_kernel(half, blocks, pairs, place_ref, factor_ref, phase_ref, own_ref, *rest):
    halo_refs = rest[:BAND]
    out_ref, raw_ref, sum_ref, box_ref, result_ref = rest[BAND:]
    tiles = half // SUB
    per_part = blocks * SUB
    per_date = 2 * per_part
    side = place_ref[0]
    lane = place_ref[1]
    low = side == 0
    row_index = lax.broadcasted_iota(jnp.int32, (SUB, LANES), 0)
    masks = []
    shifts = []
    for k in range(1, BAND + 1):
        masks.append(
            jnp.where(low, row_index - k, SUB - 1 - k - row_index) >= 0
        )
        shifts.append(jnp.where(low, SUB - k, k))

    def partners(values, edge):
        found = []
        for tile in range(tiles):
            after = values[tile + 1] if tile + 1 < tiles else edge
            before = values[tile - 1] if tile > 0 else edge
            beside = edge if tiles == 1 else jnp.where(low, after, before)
            found.append(
                [
                    pltpu.roll(jnp.where(masks[k], values[tile], beside), shifts[k], 0)
                    for k in range(BAND)
                ]
            )
        return found

    box_columns = box_ref.shape[0]
    offset = lax.broadcasted_iota(
        jnp.int32, (box_columns, LANES), 0
    ) - LOOK_COLS * lax.broadcasted_iota(jnp.int32, (box_columns, LANES), 1)
    inside = jnp.where((offset >= 0) & (offset < LOOK_COLS), 1.0, 0.0)
    box_ref[...] = inside.astype(jnp.bfloat16)

    def turned(angle, real, imag):
        cosine, sine_part = cosine_and_sine(angle)
        return real * cosine - imag * sine_part, real * sine_part + imag * cosine

    first_row = row_index < BAND
    wide = jnp.broadcast_to(factor_ref[...], (half + SUB, LANES))
    to_even = SUB // 2 * side
    to_odd = SUB // 2 - to_even
    edge_kind = 1 + 2 * BAND

    def block(t, carry):
        line_at = pl.multiple_of(t * SUB, SUB)
        column = pl.ds(pl.multiple_of(t * LANES, LANES), LANES)
        for part in range(2):
            for i in range(BAND):
                row = jnp.bitwise_xor(lane, i)
                raw_ref[part, pl.ds(row, SUB, stride=BAND), :] = halo_refs[i][
                    pl.ds(part * per_part + line_at, SUB), :
                ]
        for b in range(ROW_SETS):
            sums = {}

            def add(key, term):
                sums[key] = sums[key] + term if key in sums else term

            for even in range(b * LOOK_ROWS, (b + 1) * LOOK_ROWS, 2):
                phases = [phase_ref[line : line + 1, column] for line in (even, even + 1)]
                span = slice(even * BAND, even * BAND + SUB)
                edge = turned(
                    wide[tiles * SUB :, :] * jnp.where(first_row, *phases),
                    raw_ref[0, span, :],
                    raw_ref[1, span, :],
                )
                add((edge_kind, 0), edge[0] * edge[0] + edge[1] * edge[1])
                for line in (even, even + 1):
                    to_place = to_even if line == even else to_odd
                    edge_real, edge_imag = [pltpu.roll(v, to_place, 0) for v in edge]
                    reals = []
                    imags = []
                    for tile in range(tiles):
                        start = tile * SUB * per_date + line_at + line
                        real, imag = turned(
                            wide[tile * SUB : (tile + 1) * SUB, :]
                            * phases[line - even],
                            own_ref[pl.ds(start, SUB, stride=per_date), :],
                            own_ref[pl.ds(start + per_part, SUB, stride=per_date), :],
                        )
                        add((0, tile), real * real + imag * imag)
                        reals.append(real)
                        imags.append(imag)
                    other_reals = partners(reals, edge_real)
                    other_imags = partners(imags, edge_imag)
                    for tile in range(tiles):
                        for k in range(BAND):
                            other_real = other_reals[tile][k]
                            other_imag = other_imags[tile][k]
                            real = reals[tile]
                            imag = imags[tile]
                            add((1 + 2 * k, tile), real * other_real + imag * other_imag)
                            add((2 + 2 * k, tile), imag * other_real - real * other_imag)
            for (kind, tile), value in sums.items():
                at = sum_row(kind, b, tile)
                sum_ref[at : at + SUB, column] = value
        return carry

    def sum_row(kind, b, tile):
        return (kind * tiles * ROW_SETS + b * (1 if kind == edge_kind else tiles) + tile) * SUB

    lax.fori_loop(0, blocks, block, 0, unroll=10 if tiles == 1 else 1)

    box = box_ref[...]
    looked = None
    for part in range(sum_ref.shape[1] // box_columns):
        rest_of = sum_ref[:, part * box_columns : (part + 1) * box_columns]
        parts = None
        for piece in range(2):
            rounded = rest_of.astype(jnp.bfloat16)
            value = jnp.dot(rounded, box, preferred_element_type=jnp.float32)
            parts = value if parts is None else parts + value
            if piece < 1:
                rest_of = rest_of - rounded.astype(jnp.float32)
        if part:
            parts = pltpu.roll(parts, part * (box_columns // LOOK_COLS), 1)
        looked = parts if looked is None else looked + parts
    looked = looked * (1.0 / (LOOK_ROWS * LOOK_COLS))

    def rows_of(kind, b, tile):
        at = sum_row(kind, b, tile)
        return looked[at : at + SUB, :]

    sign = jnp.where(low, 1.0, -1.0)
    for b in range(ROW_SETS):
        powers = [rows_of(0, b, tile) for tile in range(tiles)]
        edge_power = rows_of(edge_kind, b, 0)
        other_powers = partners(powers, edge_power + pltpu.roll(edge_power, SUB // 2, 0))
        for tile in range(tiles):
            for k in range(BAND):
                look_real = rows_of(1 + 2 * k, b, tile)
                look_imag = rows_of(2 + 2 * k, b, tile) * sign
                coherence = jnp.sqrt(
                    look_real * look_real + look_imag * look_imag
                ) / jnp.sqrt((powers[tile] + EPSILON) * (other_powers[tile][k] + EPSILON))
                for kind, value in enumerate((look_real, look_imag, coherence)):
                    at = (k * half + tile * SUB) * SUB + kind * ROW_SETS + b
                    result_ref[pl.ds(at, SUB, stride=SUB), :] = value

    out_ref[...] = jnp.zeros_like(out_ref)
    result_ref[BAND * half * SUB :, :] = jnp.zeros((SUB, LANES), jnp.float32)
    for p in range(pairs):
        taken = pl.multiple_of(place_ref[2 + pairs + p] * SUB, SUB)
        out_ref[pl.ds(place_ref[2 + p] * SLOT_ROWS, SLOT_ROWS), :] = result_ref[
            pl.ds(taken, SUB), :
        ][:SLOT_ROWS]


def collect_kernel(half, got_ref, look_ref, coherence_ref):
    per_device = CAP * SLOT_ROWS
    for tile in range(half // SUB):
        for slot in range(CAP):
            for kind in range(KINDS):
                for b in range(ROW_SETS):
                    at = tile * SUB * per_device + slot * SLOT_ROWS + kind * ROW_SETS + b
                    value = got_ref[pl.ds(at, SUB, stride=per_device), :]
                    at += half * per_device
                    value += got_ref[pl.ds(at, SUB, stride=per_device), :]
                    spot = pl.ds(tile * SUB * ROW_SETS + b, SUB, stride=ROW_SETS)
                    if kind < 2:
                        look_ref[slot, kind, spot, :] = value
                    else:
                        coherence_ref[slot, spot, :] = value


def body(images, height_phase, baseline, pair_list, pair_owner):
    devices = lax.axis_size("date")
    half = devices // 2
    me = lax.axis_index("date")
    side = me // half
    lane = me % BAND
    rows, columns = images.shape[2:]
    blocks = columns // LANES
    pairs = pair_list.shape[0]
    tiles = half // SUB
    assert images.shape[0] == 1 and rows == SUB * half and half % SUB == 0
    assert columns == blocks * LANES == LANES * LOOK_COLS and blocks % BOX_PARTS == 0
    vmem = pl.BlockSpec(memory_space=pltpu.VMEM)
    smem = pl.BlockSpec(memory_space=pltpu.SMEM)
    place = jnp.stack([side, lane]).astype(jnp.int32)

    beside = lax.ppermute(height_phase, "date", [(k, k ^ 1) for k in range(devices)])

    packed = jnp.swapaxes(images[0].reshape(2, half, SUB, columns), 0, 1)
    packed = packed.reshape(half, 2 * SUB, columns)
    edges = pl.pallas_call(
        functools.partial(edge_kernel, half),
        out_shape=[jax.ShapeDtypeStruct((2 * SUB, columns), jnp.float32)] * (half // 2),
        in_specs=[pl.BlockSpec(memory_space=pltpu.HBM)],
        out_specs=[vmem] * (half // 2),
        scratch_shapes=[pltpu.SemaphoreType.DMA((half // 2,))],
        name="edge_lines",
    )(packed)
    halves = [list(range(half)), list(range(half, devices))]
    own = lax.all_to_all(
        packed, "date", split_axis=0, concat_axis=0, tiled=True, axis_index_groups=halves
    )

    def as_rows(values):
        values = values.reshape(-1, SUB, blocks, LANES)
        return jnp.swapaxes(values, 1, 2).reshape(-1, LANES)

    halos = []
    for i in range(BAND):
        arrived = None
        for g in range(half // 2 // BAND):
            steps = []
            for a in range(BAND):
                steps.append((half + a, half // 2 + BAND * g + (a ^ i)))
                steps.append((half - BAND + a, half + BAND * g + (a ^ i)))
            got = lax.ppermute(edges[BAND * g + i], "date", steps)
            arrived = got if arrived is None else arrived + got
        halos.append(as_rows(arrived))

    low = side == 0
    both = jnp.where(
        me % 2 == 0,
        jnp.concatenate([height_phase, beside]),
        jnp.concatenate([beside, height_phase]),
    )
    phase = lax.ppermute(
        both, "date", [(k, k // 2 + k % 2 * half) for k in range(devices)]
    )
    own_factors = lax.dynamic_slice_in_dim(baseline, side * half, half)
    edge_factors = lax.dynamic_slice_in_dim(
        baseline, jnp.where(low, half, half - BAND), BAND
    )
    factors = 0.5 * jnp.concatenate([own_factors, edge_factors, edge_factors])
    factors = factors[:, None]
    sums = ((1 + 2 * BAND) * tiles + 1) * ROW_SETS * SUB
    slot_rows = devices * CAP * SLOT_ROWS
    owners = pair_owner[:, 0]
    first = pair_list[:, 0]
    second = pair_list[:, 1]
    earlier = jnp.tril(owners[:, None] == owners[None, :], -1)
    slot = owners * CAP + jnp.sum(earlier.astype(jnp.int32), axis=1)
    held = (second - first - 1) * half + jnp.where(low, first, second - half)
    held = jnp.where(jnp.where(low, first < half, second >= half), held, BAND * half)
    buffer = pl.pallas_call(
        functools.partial(pair_kernel, half, blocks, pairs),
        out_shape=jax.ShapeDtypeStruct((slot_rows, LANES), jnp.float32),
        in_specs=[smem] + [vmem] * (BAND + 3),
        out_specs=vmem,
        scratch_shapes=[
            pltpu.VMEM((2, SUB * BAND, LANES), jnp.float32),
            pltpu.VMEM((sums, columns), jnp.float32),
            pltpu.VMEM((columns // BOX_PARTS, LANES), jnp.bfloat16),
            pltpu.VMEM((BAND * half * SUB + SUB, LANES), jnp.float32),
        ],
        compiler_params=pltpu.CompilerParams(vmem_limit_bytes=(12 + 12 * tiles) * MIB),
        name="pair_products",
    )(
        jnp.concatenate([place, slot, held]),
        factors,
        phase,
        as_rows(own.reshape(half * 2, SUB, columns)),
        *halos,
    )
    delivered = lax.all_to_all(
        buffer.reshape(devices, CAP * SLOT_ROWS, LANES),
        "date",
        split_axis=0,
        concat_axis=0,
        tiled=True,
    )
    look_rows = rows // LOOK_ROWS
    return pl.pallas_call(
        functools.partial(collect_kernel, half),
        out_shape=(
            jax.ShapeDtypeStruct((CAP, 2, look_rows, LANES), jnp.float32),
            jax.ShapeDtypeStruct((CAP, look_rows, LANES), jnp.float32),
        ),
        in_specs=[vmem],
        out_specs=(vmem, vmem),
        compiler_params=pltpu.CompilerParams(vmem_limit_bytes=16 * MIB),
        name="collect_slots",
    )(delivered.reshape(slot_rows, LANES))


def solution(mesh):
    in_specs = (
        P(("groups", "date"), None, None, None),
        P(("groups", "date"), None),
        P("groups"),
        P(),
        P(),
    )
    out_specs = (P(("groups", "date"), None, None, None), P(("groups", "date"), None, None))
    return jax.shard_map(body, mesh=mesh, in_specs=in_specs, out_specs=out_specs, check_vma=False)
```
